256 devices in a mesh: hst: 16 (over y_lo, z), local: 16 (over y_hi, x, core).
Axes of the slice: x: 4, y: 4 (y_hi: 2, y_lo: 2; y = y_hi * 2 + y_lo), z: 8, core: 2. Of those that a mesh axis runs over, the one named last changes fastest.
Arguments:
- hidden_in: bfloat16 [6144, 8192], P(('hst', 'local')), may hold values from -24 to 24
- cotangent: bfloat16 [6144, 8192], P(('hst', 'local')), may hold values from -6 to 6
- weight_codes: bfloat16 [8192, 8192], P('hst', 'local'), may hold values from -0.0625 to 0.0625
- block_scales: float32 [64, 64], P('hst', 'local'), may hold values from 0.3 to 3
- head_bias: float32 [8192], P('local'), may hold values from -3 to 3
Outputs:
- head_out: bfloat16 [6144, 8192], P('hst', 'local')
- grad_hidden: bfloat16 [6144, 8192], P(('hst', 'local'))
- grad_weight: float32 [8192, 8192], P('hst', 'local')
- grad_bias: float32 [8192], P('local')
The draws below stay inside these ranges and needn't reach their ends.
All inputs are finite; a program needn't handle non-finite values.
Results may differ from the reference program's by a relative error of at most 0.025.
Values may be sent and summed in bfloat16 or wider, within the bound.
No kernel may reach another device: no remote copies, remote signals or barrier semaphores. Data moves between devices by JAX's collectives and lax.ppermute only.
A program may use at most 128 MiB of HBM per device.

```python
import math
import jax
import jax.numpy as jnp
from jax import lax

D = 8192
TOK_HOST = 384
QB = 128
TOKENS = 6144
N_HST = 16
N_LOCAL = 16


def spiked(drawn, stream_key, source, target, shards_of, factor):
    owner, partner = [(jnp.arange(drawn.shape[axis_at]) // (drawn.shape[axis_at] // shards_of)).reshape([-1 if axis == axis_at else 1 for axis in range(drawn.ndim)]) for axis_at in (source, target)]
    chosen = jax.random.permutation(stream_key, shards_of)[partner]
    strong = (owner == chosen) | (owner == (partner + shards_of // 2) % shards_of)
    return jnp.where(strong, factor * drawn, drawn)


def block_levels(stream_key, shape, cuts, low, largest):
    def one(position, blocks):
        draws = jax.random.uniform(jax.random.fold_in(jax.random.fold_in(stream_key, 6), position), (blocks,), jnp.float32, low / len(cuts), largest / len(cuts))
        return jnp.repeat(jnp.exp(draws), shape[position] // blocks).reshape((-1,) + (1,) * (len(shape) - position - 1))

    gain = one(*cuts[0])
    for cut in cuts[1:]:
        gain = gain * one(*cut)
    return gain


def normal_values(rng, shape, deviation, bound, shards=(), kind=jnp.bfloat16):
    level = block_levels(rng, shape, shards, -0.22, 0.18) if shards else 1.0
    drawn = jax.random.normal(rng, shape, jnp.float32) * deviation * level
    return jnp.minimum(jnp.maximum(drawn, -bound), bound).astype(kind)


def gaussian_with(rng, shape, scale, limit, cuts, heavy, dtype=jnp.bfloat16):
    array = scale * jax.random.normal(rng, shape, jnp.float32)
    if cuts:
        array = array * block_levels(rng, shape, cuts, -0.22, 0.18)
    return jnp.clip(spiked(array, jax.random.fold_in(rng, 3), *heavy), -limit, limit).astype(dtype)


def setup_inputs(seed: int = 0) -> dict:
    keys = jax.random.split(jax.random.key(seed), 6)
    hidden_in = gaussian_with(keys[0], (TOKENS, D), 1.0, 24.0, ((0, 256),), (0, 1, 256, 6.0))
    cotangent = normal_values(keys[1], (TOKENS, D), 1.0, 6.0, ((0, 256),))
    weight_codes = normal_values(keys[2], (D, D), D ** -0.5, 0.0625, ((0, 16), (1, 16)))
    block_scales = jnp.clip(jnp.exp(math.log(3.0) - 2.3025851 * jax.random.uniform(keys[3], (D // QB, D // QB), jnp.float32) ** block_levels(keys[3], (D // QB, D // QB), ((0, 16), (1, 16)), -0.2, 0.2)), 0.3, 3.0)
    head_bias = normal_values(keys[4], (D,), 0.5, 3.0, ((0, 16),), jnp.float32)
    return {"hidden_in": hidden_in, "cotangent": cotangent, "weight_codes": weight_codes, "block_scales": block_scales, "head_bias": head_bias}


def dequantize(weight_codes, block_scales):
    row_count, col_count = weight_codes.shape
    row_blocks, col_blocks = block_scales.shape
    blocked = weight_codes.astype(jnp.float32).reshape(row_blocks, row_count // row_blocks, col_blocks, col_count // col_blocks)
    return (blocked * block_scales[:, None, :, None]).reshape(row_count, col_count).astype(jnp.bfloat16)


def silu_slope(linear):
    sigmoid_value = jax.nn.sigmoid(linear)
    return sigmoid_value * (1.0 + linear * (1.0 - sigmoid_value))


def reference(hidden_in, cotangent, weight_codes, block_scales, head_bias):
    weight = dequantize(weight_codes, block_scales)
    linear = jnp.dot(hidden_in, weight, preferred_element_type=jnp.float32) + head_bias
    head_out = (hidden_in.astype(jnp.float32) + jax.nn.silu(linear)).astype(jnp.bfloat16)
    linear_grad = (cotangent.astype(jnp.float32) * silu_slope(linear)).astype(jnp.bfloat16)
    group_width = D // N_LOCAL
    through = jnp.zeros(hidden_in.shape, jnp.float32)
    for group_index in range(N_LOCAL):
        first = group_index * group_width
        partial_sum = jnp.dot(linear_grad[:, first:first + group_width], weight[:, first:first + group_width].T, preferred_element_type=jnp.float32)
        rounded = lax.optimization_barrier(partial_sum.astype(jnp.bfloat16))
        through = through + rounded.astype(jnp.float32)
    grad_hidden = (cotangent.astype(jnp.float32) + through).astype(jnp.bfloat16)
    grad_weight = jnp.zeros((D, D), jnp.float32)
    for host_index in range(N_HST):
        first = host_index * TOK_HOST
        partial_sum = jnp.dot(hidden_in[first:first + TOK_HOST].T, linear_grad[first:first + TOK_HOST], preferred_element_type=jnp.float32)
        rounded = lax.optimization_barrier(partial_sum.astype(jnp.bfloat16))
        grad_weight = grad_weight + rounded.astype(jnp.float32)
    grad_bias = jnp.sum(linear_grad.astype(jnp.float32), 0)
    return head_out, grad_hidden, grad_weight, grad_bias
```

```python
import itertools

import jax
import jax.numpy as jnp
from jax import lax
from jax.sharding import Mesh
from jax.sharding import PartitionSpec as P

AXES = ("ylo", "z", "yhi", "x", "core")
SIZES = (2, 8, 2, 4, 2)
F32, BF16 = jnp.float32, jnp.bfloat16


def flat(ylo, z, yhi, x, core):
    return (((ylo * 8 + z) * 2 + yhi) * 4 + x) * 2 + core


def permute(value, target):
    pairs = []
    for ylo, z, yhi, x, core in itertools.product(*map(range, SIZES)):
        y_to, z_to, x_to, core_to = target(yhi * 2 + ylo, z, x, core)
        y_to, z_to, x_to = y_to % 4, z_to % 8, x_to % 4
        pairs.append(
            (flat(ylo, z, yhi, x, core), flat(y_to % 2, z_to, y_to // 2, x_to, core_to))
        )
    return lax.ppermute(value, AXES, pairs)


def shift(value, axis, step):
    return permute(
        value,
        lambda y, z, x, c: (
            y + step * (axis == "y"),
            z + step * (axis == "z"),
            x + step * (axis == "x"),
            c,
        ),
    )


def swap_cores(value):
    return permute(value, lambda y, z, x, c: (y, z, x, 1 - c))


def transpose_pair(value):
    return permute(value, lambda y, z, x, c: ((y // 2) * 2 + c, z, x, y % 2))


def flip_pair(value):
    return permute(value, lambda y, z, x, c: ((y // 2) * 2 + 1 - c, z, x, y % 2))


def dequantize(weight_codes, block_scales):
    row_count, col_count = weight_codes.shape
    row_blocks, col_blocks = block_scales.shape
    blocked = weight_codes.astype(F32).reshape(
        row_blocks, row_count // row_blocks, col_blocks, col_count // col_blocks
    )
    return (
        (blocked * block_scales[:, None, :, None]).reshape(row_count, col_count).astype(BF16)
    )


def silu_slope(linear):
    sigmoid_value = jax.nn.sigmoid(linear)
    return sigmoid_value * (1.0 + linear * (1.0 - sigmoid_value))


def ring_gather(own, axis):
    after = shift(own, axis, -1)
    before = shift(own, axis, 1)
    half = own.shape[0] // 2
    far = [shift(after[:half], axis, -1), shift(before[half:], axis, 1)]
    return [own, after, before, jnp.concatenate(far, 0)]


def ring_scatter(parts, axis):
    own, after, before, far = parts
    half = own.shape[0] // 2
    from_before = shift(far[:half], axis, 1)
    from_after = shift(far[half:], axis, -1)

    def plus(whole, low, high):
        whole = whole.astype(F32)
        if low is None:
            low = jnp.zeros_like(whole[:half])
        if high is None:
            high = jnp.zeros_like(whole[half:])
        return whole + jnp.concatenate([low.astype(F32), high.astype(F32)], 0)

    to_after = plus(after, from_before, None).astype(BF16)
    to_before = plus(before, None, from_after).astype(BF16)
    return (
        own.astype(F32)
        + shift(to_after, axis, 1).astype(F32)
        + shift(to_before, axis, -1).astype(F32)
    )


def shards(hidden_in, cotangent, weight_codes, block_scales, head_bias):
    rows, width = hidden_in.shape
    core = lax.axis_index("core")
    y_pos = lax.axis_index("yhi") * 2 + lax.axis_index("ylo")
    x_pos = lax.axis_index("x")
    y_low = lax.axis_index("ylo")
    half_width = width // 2
    quarter = half_width // 2
    block = weight_codes.shape[1]

    tile = transpose_pair(dequantize(weight_codes, block_scales))
    weight = lax.all_gather(tile, "z", axis=0, tiled=True)
    bias = jnp.where(core == y_low, head_bias, swap_cores(head_bias))

    left, right = hidden_in[:, :half_width], hidden_in[:, half_width:]
    keep = jnp.where(core == 0, left, right)
    other = swap_cores(jnp.where(core == 0, right, left))
    mine = jnp.stack([keep, other])
    x_first = jnp.stack(ring_gather(mine[:, :, :quarter], "x"))
    y_first = jnp.stack(ring_gather(mine[:, :, quarter:], "y"))
    hidden_a = jnp.stack(ring_gather(x_first, "y"))
    hidden_b = jnp.stack(ring_gather(y_first, "x"))

    def to_relative(value):
        grid = value.reshape(2, 4, 2, *value.shape[1:])
        grid = jnp.moveaxis(grid, 2, 1).reshape(4, 4, *value.shape[1:])
        for axis, pos in ((0, y_pos), (1, x_pos)):
            grid = lax.dynamic_slice_in_dim(jnp.concatenate([grid, grid], axis), pos, 4, axis)
            grid = jnp.stack([lax.index_in_dim(grid, i, axis, False) for i in (0, 1, 3, 2)], axis)
        return grid

    def from_relative(grid):
        for axis, pos in ((0, y_pos), (1, x_pos)):
            grid = jnp.stack([lax.index_in_dim(grid, i, axis, False) for i in (0, 1, 3, 2)], axis)
            grid = lax.dynamic_slice_in_dim(
                jnp.concatenate([grid, grid], axis), 4 - pos, 4, axis
            )
        return grid

    both = jnp.stack([hidden_in, cotangent]).reshape(2, rows, 16, block)
    both = lax.all_to_all(both, ("yhi", "x", "ylo"), 2, 0, tiled=True)
    both = both.reshape(16, 2, rows, block)
    hidden_cols, cotangent_cols = to_relative(both[:, 0]), to_relative(both[:, 1])

    linear_a = jnp.einsum(
        "yxcrk,kn->cyxrn", hidden_a, weight[:quarter], preferred_element_type=F32
    )
    linear_b = jnp.einsum(
        "xycrk,kn->cyxrn", hidden_b, weight[quarter:], preferred_element_type=F32
    )
    linear = linear_a + linear_b
    linear = linear[0] + swap_cores(linear[1]) + bias
    head_out = (hidden_cols.astype(F32) + jax.nn.silu(linear)).astype(BF16)
    linear_grad = (cotangent_cols.astype(F32) * silu_slope(linear)).astype(BF16)
    grads = jnp.stack([linear_grad, swap_cores(linear_grad)], 2)

    grad_a = jnp.einsum("yxcrk,yxcrn->kn", hidden_a, grads, preferred_element_type=F32)
    grad_b = jnp.einsum("xycrk,yxcrn->kn", hidden_b, grads, preferred_element_type=F32)
    grad_weight = jnp.concatenate([grad_a.astype(BF16), grad_b.astype(BF16)])
    grad_weight = lax.psum_scatter(grad_weight, "z", scatter_dimension=0, tiled=True)
    grad_weight = transpose_pair(grad_weight).astype(F32)

    through_a = jnp.einsum(
        "yxcrn,kn->yxcrk", grads, weight[:quarter], preferred_element_type=F32
    ).astype(BF16)
    through_b = jnp.einsum(
        "yxcrn,kn->xycrk", grads, weight[quarter:], preferred_element_type=F32
    ).astype(BF16)
    through_a = ring_scatter(list(through_a), "y").astype(BF16)
    through_b = ring_scatter(list(through_b), "x").astype(BF16)
    through_a = ring_scatter(list(through_a), "x")
    through_b = ring_scatter(list(through_b), "y")
    through = jnp.concatenate([through_a, through_b], 2)
    own, other = through[0], swap_cores(through[1].astype(BF16)).astype(F32)
    through = jnp.where(
        core == 0, jnp.concatenate([own, other], 1), jnp.concatenate([other, own], 1)
    )
    grad_hidden = (cotangent.astype(F32) + through).astype(BF16)

    grid = from_relative(head_out).reshape(2, 2, 4, rows, block)
    low, high = grid[:, 0], grid[:, 1]
    same = transpose_pair(jnp.where(core == 0, low, high))
    cross = flip_pair(jnp.where(core == 0, high, low))
    first = jnp.where(y_low == 0, same, cross)
    second = jnp.where(y_low == 0, cross, same)
    head_out = jnp.stack([first, second], 2).reshape(16 * rows, block)

    total = jnp.sum(linear_grad.astype(F32), (0, 1, 2))
    total = total + swap_cores(total)
    for bit in (1, 2, 4):
        total = total + permute(total, lambda y, z, x, c, bit=bit: (y, z ^ bit, x, c))
    grad_bias = transpose_pair(total)
    return head_out, grad_hidden, grad_weight, grad_bias


def solution(mesh):
    fine = Mesh(mesh.devices.reshape(SIZES), AXES)
    hst, local = ("ylo", "z"), ("yhi", "x", "core")
    in_specs = (
        P(hst + local, None),
        P(hst + local, None),
        P(hst, local),
        P(hst, local),
        P(local),
    )
    out_specs = (P(hst, local), P(hst + local, None), P(hst, local), P(local))
    return jax.shard_map(
        shards, mesh=fine, in_specs=in_specs, out_specs=out_specs, check_vma=False
    )
```

```python
import functools
import itertools

import jax
import jax.numpy as jnp
from jax import lax
from jax.experimental import pallas as pl
from jax.experimental.pallas import tpu as pltpu
from jax.sharding import Mesh
from jax.sharding import PartitionSpec as P

AXES = ("ylo", "z", "yhi", "x", "core")
SIZES = (2, 8, 2, 4, 2)
F32, BF16 = jnp.float32, jnp.bfloat16


def flat(ylo, z, yhi, x, core):
    return (((ylo * 8 + z) * 2 + yhi) * 4 + x) * 2 + core


def permute(value, target):
    pairs = []
    for ylo, z, yhi, x, core in itertools.product(*map(range, SIZES)):
        y_to, z_to, x_to, core_to = target(yhi * 2 + ylo, z, x, core)
        y_to, z_to, x_to = y_to % 4, z_to % 8, x_to % 4
        pairs.append(
            (flat(ylo, z, yhi, x, core), flat(y_to % 2, z_to, y_to // 2, x_to, core_to))
        )
    return lax.ppermute(value, AXES, pairs)


def z_shift(value, step):
    return permute(value, lambda y, z, x, c: (y, z + step, x, c))


def z_shift_transposed(value, step):
    return permute(value, lambda y, z, x, c: ((y // 2) * 2 + c, z + step, x, y % 2))


def swap_cores(value):
    return permute(value, lambda y, z, x, c: (y, z, x, 1 - c))


def transpose_pair(value):
    return z_shift_transposed(value, 0)


def flip_pair(value):
    return permute(value, lambda y, z, x, c: ((y // 2) * 2 + 1 - c, z, x, y % 2))


def near_shift(value, step):
    return permute(
        value, lambda y, z, x, c: (y + step * c, z, x + step * (1 - c), c)
    )


def far_shift(value, step):
    return permute(
        value, lambda y, z, x, c: (y + step * (1 - c), z, x + step * c, c)
    )


def dequantize(weight_codes, block_scales):
    row_count, col_count = weight_codes.shape
    row_blocks, col_blocks = block_scales.shape
    blocked = weight_codes.astype(F32).reshape(
        row_blocks, row_count // row_blocks, col_blocks, col_count // col_blocks
    )
    return (
        (blocked * block_scales[:, None, :, None]).reshape(row_count, col_count).astype(BF16)
    )


def silu_slope(linear):
    sigmoid_value = jax.nn.sigmoid(linear)
    return sigmoid_value * (1.0 + linear * (1.0 - sigmoid_value))


def ring_gather(own, shift):
    above, below = shift(own, -1), shift(own, 1)
    half = own.shape[0] // 2
    return [own, above, below, shift(above[:half], -1), shift(below[half:], 1)]


def ring_scatter(part, shift):
    far = part(2).astype(BF16)
    half = far.shape[0] // 2
    rest = ((0, 0),) * (far.ndim - 1)
    from_before = jnp.pad(shift(far[:half], 1).astype(F32), ((0, half),) + rest)
    from_after = jnp.pad(shift(far[half:], -1).astype(F32), ((half, 0),) + rest)
    to_after = shift((part(1) + from_before).astype(BF16), 1)
    to_before = shift((part(-1) + from_after).astype(BF16), -1)
    return part(0) + to_after.astype(F32) + to_before.astype(F32)


def z_gather(tile):
    above, below = z_shift_transposed(tile, -1), z_shift_transposed(tile, 1)
    tiles = {0: transpose_pair(tile), 1: above, 7: below}
    for step in (2, 3):
        above, below = z_shift(above, -1), z_shift(below, 1)
        tiles[step], tiles[8 - step] = above, below
    return tiles


EXTRA = 16


def tile_kernel(rows_in, hidden_ref, grads_ref, *refs):
    out_ref = refs[-1]
    grads = grads_ref[...]
    total = lax.dot_general(
        hidden_ref[...], grads, (((0,), (0,)), ((), ())), preferred_element_type=F32
    )
    size = total.shape[0]
    ones = jnp.ones((EXTRA, grads.shape[0]), BF16)
    bias = jnp.dot(ones, grads, preferred_element_type=F32)
    row = lax.broadcasted_iota(jnp.int32, bias.shape, 0)
    if rows_in is not None:
        first, count = rows_in
        came = refs[0]
        last = min(first + count, size)
        if first > 0:
            out_ref[:first] = total[:first].astype(BF16)
        out_ref[first:last] = (
            total[first:last] + came[: last - first].astype(F32)
        ).astype(BF16)
        if last < size:
            out_ref[last:size] = total[last:].astype(BF16)
        if first + count > size:
            sums = came[size - first :].astype(F32)
            bias = bias + sums[0:1] + sums[1:2]
    else:
        out_ref[:size] = total.astype(BF16)
    high = bias.astype(BF16).astype(F32)
    rest = jnp.where(row == 1, bias - high, 0.0)
    out_ref[size:] = jnp.where(row == 0, high, rest).astype(BF16)


def tile_part(hidden, grads, step, block, came=None, first=0, late=None):
    tokens = hidden.shape[0]
    whole = lambda value: pl.BlockSpec(value.shape, lambda i: (0,) * value.ndim)
    specs = [pl.BlockSpec((tokens, block), lambda i: (0, step)), whole(grads)]
    values = [hidden, grads]
    rows_in = None
    if came is not None:
        specs.append(whole(came))
        values.append(came)
        rows_in = (first, came.shape[0])
    if late is not None:
        specs.append(pl.BlockSpec(memory_space=pl.ANY))
        values.append(late)
    return pl.pallas_call(
        functools.partial(tile_kernel, rows_in),
        out_shape=jax.ShapeDtypeStruct((block + EXTRA, block), BF16),
        in_specs=specs,
        out_specs=pl.BlockSpec((block + EXTRA, block), lambda i: (0, 0)),
        grid=(1,),
        compiler_params=pltpu.CompilerParams(vmem_limit_bytes=24 << 20),
        cost_estimate=pl.CostEstimate(
            flops=2 * tokens * block * block, bytes_accessed=6 * tokens * block, transcendentals=0
        ),
    )(*values)


def pick_kernel(order_ref, value_ref, late_ref, out_ref):
    for i in range(out_ref.shape[0]):
        out_ref[i] = value_ref[order_ref[i]]


def pick(value, order, late):
    return pl.pallas_call(
        pick_kernel,
        out_shape=jax.ShapeDtypeStruct(value.shape, value.dtype),
        in_specs=[
            pl.BlockSpec(memory_space=pltpu.SMEM),
            pl.BlockSpec(memory_space=pltpu.VMEM),
            pl.BlockSpec(memory_space=pl.ANY),
        ],
        out_specs=pl.BlockSpec(memory_space=pltpu.VMEM),
    )(order, value, late)


def columns_kernel(which_ref, hidden_ref, late_ref, out_ref):
    out_ref[...] = hidden_ref[...]


def columns_of(hidden, which, block, late):
    tokens = hidden.shape[0]
    return pl.pallas_call(
        columns_kernel,
        out_shape=jax.ShapeDtypeStruct((tokens, block), hidden.dtype),
        grid_spec=pltpu.PrefetchScalarGridSpec(
            num_scalar_prefetch=1,
            grid=(1,),
            in_specs=[
                pl.BlockSpec((tokens, block), lambda i, which: (0, which[0])),
                pl.BlockSpec(memory_space=pl.ANY),
            ],
            out_specs=pl.BlockSpec((tokens, block), lambda i, which: (0, 0)),
        ),
    )(which, hidden, late)


def z_scatter(hidden, grads, block):
    part = functools.partial(tile_part, hidden, grads, block=block)
    far = part(4)
    half = block // 2
    up, down = z_shift(far[:half], 1), z_shift(far[half:], -1)
    arrived = [up]
    up, down = z_shift(part(3, came=up), 1), z_shift(part(5, came=down, first=half), -1)
    arrived.append(up)
    up, down = z_shift(part(2, came=up), 1), z_shift(part(6, came=down), -1)
    own = transpose_pair(part(0, late=arrived[0]))
    up, down = part(1, came=up), part(7, came=down)
    up, down = z_shift_transposed(up, 1), z_shift_transposed(down, -1)
    total = up.astype(F32) + down.astype(F32) + own.astype(F32)
    return total[:block], total[block] + total[block + 1], arrived


def direct_gather(own, shift):
    return [own, shift(own, -1), shift(own, 1), shift(own, 2)]


def direct_scatter(part, shift):
    sent = [shift(part(d).astype(BF16), d) for d in (2, 1, -1)]
    return part(0) + sum(value.astype(F32) for value in sent)


def roll(value, first, axis):
    size = value.shape[axis]
    return lax.dynamic_slice_in_dim(jnp.concatenate([value, value], axis), first, size, axis)


def reorder(grid, axis):
    return jnp.concatenate(
        [lax.slice_in_dim(grid, i, i + 1, axis=axis) for i in (0, 1, 3, 2)], axis
    )


def shards(hidden_in, cotangent, weight_codes, block_scales, head_bias):
    rows, width = hidden_in.shape
    core = lax.axis_index("core")
    y_low, y_high = lax.axis_index("ylo"), lax.axis_index("yhi")
    y_pos, x_pos, z_pos = y_high * 2 + y_low, lax.axis_index("x"), lax.axis_index("z")
    half_width = width // 2
    block = weight_codes.shape[1]

    tiles = z_gather(dequantize(weight_codes, block_scales))
    bias = jnp.where(core == y_low, head_bias, swap_cores(head_bias))

    def half_features(which):
        part = lax.dynamic_slice_in_dim(hidden_in, which * half_width, half_width, 1)
        return roll(part, z_pos * block, 1)

    mine = jnp.stack([half_features(core), swap_cores(half_features(1 - core))])
    near = ring_gather(mine, near_shift)
    near = jnp.concatenate([jnp.stack(near[:3]), jnp.concatenate(near[3:])[None]])
    pieces = ring_gather(near, far_shift)
    half = block // 2
    last = [
        z_shift(tiles[3][:half], -1),
        z_shift(tiles[5][half:], 1),
    ]
    tiles = [tiles[i] for i in range(4)] + last + [tiles[i] for i in (5, 6, 7)]
    weight = jnp.concatenate(tiles)
    hidden = jnp.concatenate(pieces).reshape(16 * 2 * rows, half_width)

    distances = jnp.array([0, 1, 3, 2])
    y_all, x_all = (y_pos + distances) % 4, (x_pos + distances) % 4
    index = y_all[:, None] // 2 * 8 + x_all[None, :] * 2 + y_all[:, None] % 2
    index = jnp.where(core == 0, index, index.T).reshape(16).astype(jnp.int32)
    columns = jnp.swapaxes(cotangent.reshape(rows, 16, block), 0, 1)
    columns = lax.all_to_all(columns, ("yhi", "x", "ylo"), 0, 0, tiled=True)
    columns = pick(columns, index, pieces[1]).reshape(4, 4, rows, block)

    def own_order(grid):
        return jnp.where(core == 0, grid, jnp.swapaxes(grid, 0, 1))

    linear = jnp.concatenate(
        [jnp.einsum("acrk,kn->acrn", p, weight, preferred_element_type=F32) for p in pieces]
    ).reshape(4, 4, 2, rows, block)
    other = jnp.swapaxes(swap_cores(linear[:, :, 1]), 0, 1)
    linear = linear[:, :, 0] + other + bias
    linear_grad = (columns.astype(F32) * silu_slope(linear)).astype(BF16)
    other = jnp.swapaxes(swap_cores(linear_grad), 0, 1)
    grads = jnp.stack([linear_grad, other], 2)

    grad_weight, grad_bias, arrived = z_scatter(
        hidden, grads.reshape(-1, block), block
    )

    through = jnp.einsum("abcrn,kn->abcrk", grads, weight, preferred_element_type=F32)
    through = through.astype(BF16)
    through_far = through
    through = ring_scatter(
        lambda d: through_far[(0, 1, 3, 2)[d % 4]].astype(F32), far_shift
    ).astype(BF16)
    through_near = through
    through = direct_scatter(
        lambda d: through_near[(0, 1, 3, 2)[d % 4]].astype(F32), near_shift
    )
    through = jnp.stack([through[0].astype(BF16), swap_cores(through[1].astype(BF16))])
    through = roll(through, (8 - z_pos) % 8 * block, 2).astype(F32)
    through = jnp.where(
        core == 0,
        jnp.concatenate([through[0], through[1]], 1),
        jnp.concatenate([through[1], through[0]], 1),
    )
    grad_hidden = (cotangent.astype(F32) + through).astype(BF16)

    which = ((x_pos * 2 + y_low + 8 - z_pos) % 8).astype(jnp.int32).reshape(1)
    columns = columns_of(hidden, which, block, arrived[1]).reshape(4, 4, 2, rows, block)
    other = jnp.swapaxes(swap_cores(columns[:, :, 1]), 0, 1)
    columns = jnp.where(core == y_high, columns[:, :, 0], other)
    head_out = (columns.astype(F32) + jax.nn.silu(linear)).astype(BF16)
    grid = reorder(reorder(own_order(head_out), 0), 1)
    grid = roll(roll(grid, (4 - y_pos) % 4, 0), (4 - x_pos) % 4, 1)
    grid = grid.reshape(2, 2, 4, rows, block)
    low, high = grid[:, 0], grid[:, 1]
    same = transpose_pair(jnp.where(core == 0, low, high))
    cross = flip_pair(jnp.where(core == 0, high, low))
    head_out = jnp.where(
        y_low == 0, jnp.stack([same, cross], 2), jnp.stack([cross, same], 2)
    ).reshape(16 * rows, block)

    return head_out, grad_hidden, grad_weight, grad_bias


def solution(mesh):
    fine = Mesh(mesh.devices.reshape(SIZES), AXES)
    hst, local = ("ylo", "z"), ("yhi", "x", "core")
    in_specs = (
        P(hst + local, None),
        P(hst + local, None),
        P(hst, local),
        P(hst, local),
        P(local),
    )
    out_specs = (P(hst, local), P(hst + local, None), P(hst, local), P(local))
    return jax.shard_map(
        shards, mesh=fine, in_specs=in_specs, out_specs=out_specs, check_vma=False
    )
```

```python
import functools
import itertools

import jax
import jax.numpy as jnp
from jax import lax
from jax.experimental import pallas as pl
from jax.experimental.pallas import tpu as pltpu
from jax.sharding import Mesh
from jax.sharding import PartitionSpec as P

AXES = ("ylo", "z", "yhi", "x", "core")
SIZES = (2, 8, 2, 4, 2)
F32, BF16 = jnp.float32, jnp.bfloat16


def flat(ylo, z, yhi, x, core):
    return (((ylo * 8 + z) * 2 + yhi) * 4 + x) * 2 + core


def permute(value, target):
    pairs = []
    for ylo, z, yhi, x, core in itertools.product(*map(range, SIZES)):
        y_to, z_to, x_to, core_to = target(yhi * 2 + ylo, z, x, core)
        y_to, z_to, x_to = y_to % 4, z_to % 8, x_to % 4
        pairs.append(
            (flat(ylo, z, yhi, x, core), flat(y_to % 2, z_to, y_to // 2, x_to, core_to))
        )
    return lax.ppermute(value, AXES, pairs)


def z_shift(value, step):
    return permute(value, lambda y, z, x, c: (y, z + step, x, c))


def z_shift_transposed(value, step):
    return permute(value, lambda y, z, x, c: ((y // 2) * 2 + c, z + step, x, y % 2))


def swap_cores(value):
    return permute(value, lambda y, z, x, c: (y, z, x, 1 - c))


def transpose_pair(value):
    return z_shift_transposed(value, 0)


def flip_pair(value):
    return permute(value, lambda y, z, x, c: ((y // 2) * 2 + 1 - c, z, x, y % 2))


def near_shift(value, step):
    return permute(
        value, lambda y, z, x, c: (y + step * c, z, x + step * (1 - c), c)
    )


def far_shift(value, step):
    return permute(
        value, lambda y, z, x, c: (y + step * (1 - c), z, x + step * c, c)
    )


def dequantize(weight_codes, block_scales):
    row_count, col_count = weight_codes.shape
    row_blocks, col_blocks = block_scales.shape
    blocked = weight_codes.astype(F32).reshape(
        row_blocks, row_count // row_blocks, col_blocks, col_count // col_blocks
    )
    return (
        (blocked * block_scales[:, None, :, None]).reshape(row_count, col_count).astype(BF16)
    )


def silu_slope(linear):
    sigmoid_value = jax.nn.sigmoid(linear)
    return sigmoid_value * (1.0 + linear * (1.0 - sigmoid_value))


def ring_gather(own, shift):
    above, below = shift(own, -1), shift(own, 1)
    half = own.shape[0] // 2
    return [own, above, below, shift(above[:half], -1), shift(below[half:], 1)]


def ring_scatter(part, shift):
    far = part(2).astype(BF16)
    half = far.shape[0] // 2
    rest = ((0, 0),) * (far.ndim - 1)
    from_before = jnp.pad(shift(far[:half], 1).astype(F32), ((0, half),) + rest)
    from_after = jnp.pad(shift(far[half:], -1).astype(F32), ((half, 0),) + rest)
    to_after = shift((part(1) + from_before).astype(BF16), 1)
    to_before = shift((part(-1) + from_after).astype(BF16), -1)
    return part(0) + to_after.astype(F32) + to_before.astype(F32)


def z_gather(tile):
    above, below = z_shift_transposed(tile, -1), z_shift_transposed(tile, 1)
    tiles = {0: transpose_pair(tile), 1: above, 7: below}
    for step in (2, 3):
        above, below = z_shift(above, -1), z_shift(below, 1)
        tiles[step], tiles[8 - step] = above, below
    return tiles


EXTRA = 16


def tile_kernel(rows_in, hidden_ref, grads_ref, *refs):
    out_ref = refs[-1]
    grads = grads_ref[...]
    total = lax.dot_general(
        hidden_ref[...], grads, (((0,), (0,)), ((), ())), preferred_element_type=F32
    )
    size = total.shape[0]
    ones = jnp.ones((EXTRA, grads.shape[0]), BF16)
    bias = jnp.dot(ones, grads, preferred_element_type=F32)
    row = lax.broadcasted_iota(jnp.int32, bias.shape, 0)
    if rows_in is not None:
        first, count = rows_in
        came = refs[0]
        last = min(first + count, size)
        if first > 0:
            out_ref[:first] = total[:first].astype(BF16)
        out_ref[first:last] = (
            total[first:last] + came[: last - first].astype(F32)
        ).astype(BF16)
        if last < size:
            out_ref[last:size] = total[last:].astype(BF16)
        if first + count > size:
            sums = came[size - first :].astype(F32)
            bias = bias + sums[0:1] + sums[1:2]
    else:
        out_ref[:size] = total.astype(BF16)
    high = bias.astype(BF16).astype(F32)
    rest = jnp.where(row == 1, bias - high, 0.0)
    out_ref[size:] = jnp.where(row == 0, high, rest).astype(BF16)


def tile_part(hidden, grads, step, block, came=None, first=0, late=()):
    tokens = hidden.shape[0]
    whole = lambda value: pl.BlockSpec(value.shape, lambda i: (0,) * value.ndim)
    specs = [pl.BlockSpec((tokens, block), lambda i: (0, step)), whole(grads)]
    values = [hidden, grads]
    rows_in = None
    if came is not None:
        specs.append(whole(came))
        values.append(came)
        rows_in = (first, came.shape[0])
    for value in late:
        specs.append(pl.BlockSpec(memory_space=pl.ANY))
        values.append(value)
    return pl.pallas_call(
        functools.partial(tile_kernel, rows_in),
        out_shape=jax.ShapeDtypeStruct((block + EXTRA, block), BF16),
        in_specs=specs,
        out_specs=pl.BlockSpec((block + EXTRA, block), lambda i: (0, 0)),
        grid=(1,),
        compiler_params=pltpu.CompilerParams(vmem_limit_bytes=24 << 20),
        cost_estimate=pl.CostEstimate(
            flops=2 * tokens * block * block, bytes_accessed=6 * tokens * block, transcendentals=0
        ),
    )(*values)


def pick_kernel(order_ref, value_ref, late_ref, out_ref):
    for i in range(out_ref.shape[0]):
        out_ref[i] = value_ref[order_ref[i]]


def pick(value, order, late):
    return pl.pallas_call(
        pick_kernel,
        out_shape=jax.ShapeDtypeStruct(value.shape, value.dtype),
        in_specs=[
            pl.BlockSpec(memory_space=pltpu.SMEM),
            pl.BlockSpec(memory_space=pltpu.VMEM),
            pl.BlockSpec(memory_space=pl.ANY),
        ],
        out_specs=pl.BlockSpec(memory_space=pltpu.VMEM),
    )(order, value, late)


def columns_kernel(which_ref, hidden_ref, late_ref, out_ref):
    out_ref[...] = hidden_ref[...]


def columns_of(hidden, which, block, late):
    tokens = hidden.shape[0]
    return pl.pallas_call(
        columns_kernel,
        out_shape=jax.ShapeDtypeStruct((tokens, block), hidden.dtype),
        grid_spec=pltpu.PrefetchScalarGridSpec(
            num_scalar_prefetch=1,
            grid=(1,),
            in_specs=[
                pl.BlockSpec((tokens, block), lambda i, which: (0, which[0])),
                pl.BlockSpec(memory_space=pl.ANY),
            ],
            out_specs=pl.BlockSpec((tokens, block), lambda i, which: (0, 0)),
        ),
    )(which, hidden, late)


def z_scatter(hidden, grads, block, which):
    part = functools.partial(tile_part, hidden, grads, block=block)
    far = part(4)
    half = block // 2
    up, down = z_shift(far[:half], 1), z_shift(far[half:], -1)
    columns = columns_of(hidden, which, block, far)
    up, down = part(3, came=up, late=(columns, down)), part(5, came=down, first=half, late=(up,))
    up, down = z_shift(up, 1), z_shift(down, -1)
    own = transpose_pair(part(0, late=(columns,)))
    up, down = z_shift(part(2, came=up, late=(own,)), 1), z_shift(part(6, came=down), -1)
    up, down = part(1, came=up), part(7, came=down)
    up, down = z_shift_transposed(up, 1), z_shift_transposed(down, -1)
    total = up.astype(F32) + down.astype(F32) + own.astype(F32)
    return total[:block], total[block] + total[block + 1], columns


def direct_gather(own, shift):
    return [own, shift(own, -1), shift(own, 1), shift(own, 2)]


def direct_scatter(part, shift):
    sent = [shift(part(d).astype(BF16), d) for d in (2, 1, -1)]
    return part(0) + sum(value.astype(F32) for value in sent)


def roll(value, first, axis):
    size = value.shape[axis]
    return lax.dynamic_slice_in_dim(jnp.concatenate([value, value], axis), first, size, axis)


def reorder(grid, axis):
    return jnp.concatenate(
        [lax.slice_in_dim(grid, i, i + 1, axis=axis) for i in (0, 1, 3, 2)], axis
    )


def shards(hidden_in, cotangent, weight_codes, block_scales, head_bias):
    rows, width = hidden_in.shape
    core = lax.axis_index("core")
    y_low, y_high = lax.axis_index("ylo"), lax.axis_index("yhi")
    y_pos, x_pos, z_pos = y_high * 2 + y_low, lax.axis_index("x"), lax.axis_index("z")
    half_width = width // 2
    block = weight_codes.shape[1]

    tiles = z_gather(dequantize(weight_codes, block_scales))
    bias = jnp.where(core == y_low, head_bias, swap_cores(head_bias))

    def half_features(which):
        part = lax.dynamic_slice_in_dim(hidden_in, which * half_width, half_width, 1)
        return roll(part, z_pos * block, 1)

    mine = jnp.stack([half_features(core), swap_cores(half_features(1 - core))])
    near = ring_gather(mine, near_shift)
    near = jnp.concatenate([jnp.stack(near[:3]), jnp.concatenate(near[3:])[None]])
    pieces = ring_gather(near, far_shift)
    half = block // 2
    last = [
        z_shift(tiles[3][:half], -1),
        z_shift(tiles[5][half:], 1),
    ]
    tiles = [tiles[i] for i in range(4)] + last + [tiles[i] for i in (5, 6, 7)]
    weight = jnp.concatenate(tiles)
    hidden = jnp.concatenate(pieces).reshape(16 * 2 * rows, half_width)

    distances = jnp.array([0, 1, 3, 2])
    y_all, x_all = (y_pos + distances) % 4, (x_pos + distances) % 4
    index = y_all[:, None] // 2 * 8 + x_all[None, :] * 2 + y_all[:, None] % 2
    index = jnp.where(core == 0, index, index.T).reshape(16).astype(jnp.int32)
    columns = jnp.swapaxes(cotangent.reshape(rows, 16, block), 0, 1)
    columns = lax.all_to_all(columns, ("yhi", "x", "ylo"), 0, 0, tiled=True)
    columns = pick(columns, index, pieces[1]).reshape(4, 4, rows, block)

    def own_order(grid):
        return jnp.where(core == 0, grid, jnp.swapaxes(grid, 0, 1))

    linear = jnp.concatenate(
        [jnp.einsum("acrk,kn->acrn", p, weight, preferred_element_type=F32) for p in pieces]
    ).reshape(4, 4, 2, rows, block)
    other = jnp.swapaxes(swap_cores(linear[:, :, 1]), 0, 1)
    linear = linear[:, :, 0] + other + bias
    linear_grad = (columns.astype(F32) * silu_slope(linear)).astype(BF16)
    other = jnp.swapaxes(swap_cores(linear_grad), 0, 1)
    grads = jnp.stack([linear_grad, other], 2)

    which = ((x_pos * 2 + y_low + 8 - z_pos) % 8).astype(jnp.int32).reshape(1)
    grad_weight, grad_bias, columns = z_scatter(hidden, grads.reshape(-1, block), block, which)

    through = jnp.einsum("abcrn,kn->abcrk", grads, weight, preferred_element_type=F32)
    through = through.astype(BF16)
    through_far = through
    through = ring_scatter(
        lambda d: through_far[(0, 1, 3, 2)[d % 4]].astype(F32), far_shift
    ).astype(BF16)
    through_near = through
    through = direct_scatter(
        lambda d: through_near[(0, 1, 3, 2)[d % 4]].astype(F32), near_shift
    )
    through = jnp.stack([through[0].astype(BF16), swap_cores(through[1].astype(BF16))])
    through = roll(through, (8 - z_pos) % 8 * block, 2).astype(F32)
    through = jnp.where(
        core == 0,
        jnp.concatenate([through[0], through[1]], 1),
        jnp.concatenate([through[1], through[0]], 1),
    )
    grad_hidden = (cotangent.astype(F32) + through).astype(BF16)

    columns = columns.reshape(4, 4, 2, rows, block)
    other = jnp.swapaxes(swap_cores(columns[:, :, 1]), 0, 1)
    columns = jnp.where(core == y_high, columns[:, :, 0], other)
    head_out = (columns.astype(F32) + jax.nn.silu(linear)).astype(BF16)
    grid = reorder(reorder(own_order(head_out), 0), 1)
    grid = roll(roll(grid, (4 - y_pos) % 4, 0), (4 - x_pos) % 4, 1)
    grid = grid.reshape(2, 2, 4, rows, block)
    low, high = grid[:, 0], grid[:, 1]
    same = transpose_pair(jnp.where(core == 0, low, high))
    cross = flip_pair(jnp.where(core == 0, high, low))
    head_out = jnp.where(
        y_low == 0, jnp.stack([same, cross], 2), jnp.stack([cross, same], 2)
    ).reshape(16 * rows, block)

    return head_out, grad_hidden, grad_weight, grad_bias


def solution(mesh):
    fine = Mesh(mesh.devices.reshape(SIZES), AXES)
    hst, local = ("ylo", "z"), ("yhi", "x", "core")
    in_specs = (
        P(hst + local, None),
        P(hst + local, None),
        P(hst, local),
        P(hst, local),
        P(local),
    )
    out_specs = (P(hst, local), P(hst + local, None), P(hst, local), P(local))
    return jax.shard_map(
        shards, mesh=fine, in_specs=in_specs, out_specs=out_specs, check_vma=False
    )
```
